32 devices in a mesh: row: 4 (over y, x), col: 8 (over z, core).
Axes of the slice: x: 2, y: 2, z: 4, core: 2. Of those that a mesh axis runs over, the one named last changes fastest.
Arguments:
- galaxy: float32 [128, 256, 256], P('row', 'col'), may hold values from 0.03 to 32, as said below
- randoms: float32 [128, 256, 256], P('row', 'col'), may hold values from 0.5 to 4
- coverage: int32 [128, 256, 256], P('row', 'col'), may hold values from 0 to 1
- patch: int32 [128, 256, 256], P('row', 'col'), may hold values from 0 to 127
Outputs:
- contrast: float32 [128, 256, 256], P('row', 'col')
- patch_sums: float32 [4, 128], replicated
The draws below stay inside these ranges and needn't reach their ends.
Inputs may be any that keep to these rules, and one draw needn't show every extreme that they name: `galaxy`: positive densities.
All inputs are finite; a program needn't handle non-finite values.
Results may differ from the reference program's by a relative error of at most 0.00016.
Values sent between devices are 32-bit elements; how exact they have to be, the bound alone decides.
A program may use at most 64 MiB of HBM per device.

```python
import math
import jax
import jax.numpy as jnp

NZ = 256
RADIUS = 16
NPATCH = 128
NX = 128
NY = 256


def line_factor(key, count):
    logs = jax.random.uniform(key, (count,), jnp.float32, jnp.log(0.4), jnp.log(2.5))
    return jnp.exp(logs)


def draw_galaxy(key, part):
    keys = jax.random.split(jax.random.fold_in(key, 11), 4)
    base_logs = jax.random.uniform(keys[0], (NX, NY, NZ), jnp.float32, jnp.log(0.5), jnp.log(2.0))
    base = jnp.exp(base_logs)
    along_x = line_factor(keys[1], NX)[:, None, None]
    along_y = line_factor(keys[2], NY)[None, :, None]
    along_z = line_factor(keys[3], NZ)[None, None, :]
    return (base * along_x * along_y * along_z).astype(jnp.float32)


def draw_coverage(key, part):
    keys = jax.random.split(key, 4)
    centre_x = jax.random.randint(keys[0], (), NX // 4, 3 * NX // 4 + 1)
    centre_y = jax.random.randint(keys[1], (), NY // 4, 3 * NY // 4 + 1)
    radius = jax.random.randint(keys[2], (), 200, 350)
    xpos = jnp.arange(NX, dtype=jnp.int32)[:, None, None]
    ypos = jnp.arange(NY, dtype=jnp.int32)[None, :, None]
    upos = (xpos - centre_x) * 1024 // NX
    vpos = (ypos - centre_y) * 1024 // NY
    outside = upos * upos + vpos * vpos >= radius * radius
    holes = jax.random.randint(keys[3], (NX, NY, NZ), 0, 8) > 0
    return (outside & holes).astype(jnp.int32)


def draw_patch(key, part):
    keys = jax.random.split(key, 4)
    shift_x = jax.random.randint(keys[0], (), 0, NX)
    shift_y = jax.random.randint(keys[1], (), 0, NY)
    xpos = (jnp.arange(NX, dtype=jnp.int32) + shift_x) % NX
    ypos = (jnp.arange(NY, dtype=jnp.int32) + shift_y) % NY
    tile = xpos[:, None] // (NX // 8) * (NPATCH // 8) + ypos[None, :] // (NY // 16) * (NPATCH // 128)
    tile = jnp.broadcast_to(tile[:, :, None], (NX, NY, NZ))
    spread = jax.random.randint(keys[2], (NX, NY, NZ), 0, NPATCH)
    relabel = jax.random.randint(keys[3], (NX, NY, NZ), 0, 8) == 0
    return jnp.where(relabel, spread, tile).astype(jnp.int32)


def level_of(key, extent, pieces, smallest, top_value):
    def one(axis_at, shards_of):
        steps = jax.random.uniform(jax.random.fold_in(jax.random.fold_in(key, 6), axis_at), (shards_of,), jnp.float32, smallest / len(pieces), top_value / len(pieces))
        return jnp.repeat(jnp.exp(steps), extent[axis_at] // shards_of).reshape((-1,) + (1,) * (len(extent) - axis_at - 1))

    factor_of = one(*pieces[0])
    for cut in pieces[1:]:
        factor_of = factor_of * one(*cut)
    return factor_of


def setup_inputs(seed: int = 0) -> dict:
    key_of = jax.random.split(jax.random.key(seed), 5)
    galaxy = draw_galaxy(jax.random.fold_in(key_of[4], 71), 0)
    randoms = jnp.clip(jnp.exp(math.log(4.0) - 2.0794415 * jax.random.uniform(key_of[1], (NX, NY, NZ), jnp.float32) ** level_of(key_of[1], (NX, NY, NZ), ((0, 4), (1, 8)), -0.2, 0.2)), 0.5, 4.0)
    coverage = draw_coverage(jax.random.fold_in(key_of[4], 71), 0)
    patch = draw_patch(jax.random.fold_in(key_of[4], 71), 0)
    return {"galaxy": galaxy, "randoms": randoms, "coverage": coverage, "patch": patch}


def kernel_taps():
    offs = jnp.arange(-RADIUS, RADIUS + 1).astype(jnp.float32)
    sigma = RADIUS / 2.0
    vals = jnp.exp(-offs * offs / (2.0 * sigma * sigma))
    return vals / jnp.sum(vals)


def smooth_axis(field, taps, axis):
    width = [(0, 0)] * field.ndim
    width[axis] = (RADIUS, RADIUS)
    padded = jnp.pad(field, width)
    count = field.shape[axis]
    total = jnp.zeros_like(field)
    for j in range(2 * RADIUS + 1):
        total = total + taps[j] * lax_slice(padded, j, count, axis)
    return total


def lax_slice(padded, start, count, axis):
    return jax.lax.slice_in_dim(padded, start, start + count, axis=axis)


def reference(galaxy, randoms, coverage, patch):
    taps = kernel_taps()

    def smooth(field):
        return smooth_axis(smooth_axis(smooth_axis(field, taps, 2), taps, 0), taps, 1)

    gal_s = smooth(galaxy)
    ran_s = smooth(randoms)
    weightm = coverage.astype(jnp.float32)
    alpha = jnp.sum(weightm * galaxy) / jnp.sum(weightm * randoms)
    nbar = alpha * ran_s
    weight = 1.0 / (1.0 + 2.0 * nbar)
    contrast = weightm * weight * (gal_s / nbar - 1.0)
    flat_m = weightm.reshape(-1)
    flat_c = contrast.reshape(-1)
    powers = jnp.stack([flat_m, flat_m * flat_c, flat_m * flat_c * flat_c, flat_m * flat_c * flat_c * flat_c], axis=1)
    sums = jax.ops.segment_sum(powers, patch.reshape(-1), num_segments=NPATCH)
    scale = NPATCH / (NX * NY * NZ)
    return contrast, (sums.T * scale).astype(jnp.float32)
```

```python
import functools

import jax
import jax.numpy as jnp
import ml_dtypes
import numpy as np
from jax import lax
from jax.experimental import pallas as pl
from jax.experimental.pallas import tpu as pltpu
from jax.sharding import PartitionSpec as P

RADIUS = 16
NPATCH = 128
LANES = 128
F32 = jnp.float32
BF16 = jnp.bfloat16
MESH = pl.DeviceIdType.MESH


def taps_np():
    offs = np.arange(-RADIUS, RADIUS + 1).astype(np.float32)
    sigma = RADIUS / 2.0
    vals = np.exp(-offs * offs / np.float32(2.0 * sigma * sigma)).astype(np.float32)
    return (vals / vals.sum(dtype=np.float32)).astype(np.float32)


def split_np(mat):
    high = mat.astype(ml_dtypes.bfloat16)
    low = (mat - high.astype(np.float32)).astype(ml_dtypes.bfloat16)
    return high, low


def band(outs, ins, shift):
    taps = taps_np()
    mat = np.zeros((outs, ins), np.float32)
    for o in range(outs):
        for j in range(-RADIUS, RADIUS + 1):
            i = o + j + shift
            if 0 <= i < ins:
                mat[o, i] = taps[j + RADIUS]
    return mat


def split(val):
    high = val.astype(BF16)
    low = (val - high.astype(F32)).astype(BF16)
    return high, low


def dot(a, b):
    return jnp.dot(a, b, preferred_element_type=F32)


def gather_sum(axis, size, buf, send, recv):
    me = lax.axis_index(axis)
    copies = []
    for k in range(1, size):
        copy = pltpu.make_async_remote_copy(
            src_ref=buf.at[me],
            dst_ref=buf.at[me],
            send_sem=send.at[k - 1],
            recv_sem=recv.at[k - 1],
            device_id={axis: lax.rem(me + k, size)},
            device_id_type=MESH,
        )
        copy.start()
        copies.append(copy)
    return copies


def add_up(copies, buf, size):
    for copy in copies:
        copy.wait()
    total = buf[0]
    for k in range(1, size):
        total = total + buf[k]
    return total


def kernel(
    rows, cols, scale,
    gal, ran, cov, pat, thi, tlo, kxhi, kxlo, kyhi, kylo, rep,
    contrast, sums,
    xb, yb, acc, trow, tcol, srow, scol,
    sx, rx, sy, ry, s1, r1, s2, r2, s3, r3, s4, r4,
):
    X, Y, Z = gal.shape
    halves = Z // LANES
    W = RADIUS
    me_r = lax.axis_index("row")
    me_c = lax.axis_index("col")

    barrier = pltpu.get_barrier_semaphore()
    for k in range(1, rows):
        pl.semaphore_signal(barrier, inc=1, device_id={"row": lax.rem(me_r + k, rows)}, device_id_type=MESH)
    for k in range(1, cols):
        pl.semaphore_signal(barrier, inc=1, device_id={"col": lax.rem(me_c + k, cols)}, device_id_type=MESH)
    pl.semaphore_wait(barrier, rows + cols - 2)

    def xcopy(h, up):
        own, far = ((X, 0) if up else (W, X + W))
        return pltpu.make_async_remote_copy(
            src_ref=xb.at[h, :, pl.ds(own, W)],
            dst_ref=xb.at[h, :, pl.ds(far, W)],
            send_sem=sx.at[h, int(up)],
            recv_sem=rx.at[h, int(up)],
            device_id={"row": lax.rem(me_r + (1 if up else rows - 1), rows)},
            device_id_type=MESH,
        )

    def ycopy(h, up):
        own, far = ((Y, 0) if up else (W, Y + W))
        return pltpu.make_async_remote_copy(
            src_ref=yb.at[h, :, :, pl.ds(own, W)],
            dst_ref=yb.at[h, :, :, pl.ds(far, W)],
            send_sem=sy.at[h, int(up)],
            recv_sem=ry.at[h, int(up)],
            device_id={"col": lax.rem(me_c + (1 if up else cols - 1), cols)},
            device_id_type=MESH,
        )

    PX = 8
    for h in range(halves):
        lanes = pl.ds(h * LANES, LANES)

        def zstep(i, unused):
            for f, ref in enumerate((gal, ran)):
                high, low = split(ref[pl.ds(i * PX, PX)].reshape(PX * Y, Z))
                th = thi[:, lanes]
                val = dot(high, th) + dot(high, tlo[:, lanes]) + dot(low, th)
                xb[h, f, pl.ds(W + i * PX, PX)] = val.reshape(PX, Y, LANES)
            return unused

        lax.fori_loop(0, X // PX, zstep, 0)

        @pl.when(me_r > 0)
        def _():
            xcopy(h, False).start()

        @pl.when(me_r < rows - 1)
        def _():
            xcopy(h, True).start()

        @pl.when(me_r == 0)
        def _():
            xb[h, :, 0:W] = jnp.zeros((2, W, Y, LANES), F32)

        @pl.when(me_r == rows - 1)
        def _():
            xb[h, :, X + W:] = jnp.zeros((2, W, Y, LANES), F32)

        @pl.when(me_c == 0)
        def _():
            yb[h, :, :, 0:W] = jnp.zeros((2, X, W, LANES), F32)

        @pl.when(me_c == cols - 1)
        def _():
            yb[h, :, :, Y + W:] = jnp.zeros((2, X, W, LANES), F32)

    def tstep(i, carry):
        m = cov[i].astype(F32)
        g = (m * gal[i]).reshape(Y // 8, 8, Z).sum(axis=0)
        r = (m * ran[i]).reshape(Y // 8, 8, Z).sum(axis=0)
        return carry[0] + g, carry[1] + r

    zero = jnp.zeros((8, Z), F32)
    tg, tr = lax.fori_loop(0, X, tstep, (zero, zero))
    for f, t in enumerate((tg, tr)):
        trow[me_r, f] = sum(t[:, k * LANES:(k + 1) * LANES] for k in range(Z // LANES))
    tcol[me_c] = add_up(gather_sum("row", rows, trow, s1, r1), trow, rows)
    tot = add_up(gather_sum("col", cols, tcol, s2, r2), tcol, cols)
    alpha = jnp.sum(tot[0], keepdims=True) / jnp.sum(tot[1], keepdims=True)

    acc[...] = jnp.zeros_like(acc)
    iota_hi = lax.broadcasted_iota(jnp.int32, (8, 2 * LANES), 0)
    iota_lo = lax.broadcasted_iota(jnp.int32, (16, 2 * LANES), 0)

    def finish(h):
        lanes = pl.ds(h * LANES, LANES)

        def cstep(i, unused):
            x4 = pl.ds(i * 4, 4)
            both = jnp.concatenate(
                [yb[h, f, x4].reshape(4 * (Y + 2 * W), LANES) for f in range(2)], axis=1
            )
            high, low = split(both)
            kh = kyhi[...]
            val = dot(kh, high) + dot(kylo[...], high) + dot(kh, low)
            m = cov[x4, :, lanes].astype(F32).reshape(4 * Y, LANES)
            nbar = alpha * val[:, LANES:]
            weight = 1.0 / (1.0 + 2.0 * nbar)
            c = m * weight * (val[:, :LANES] / nbar - 1.0)
            contrast[x4, :, lanes] = c.reshape(4, Y, LANES)
            return unused

        lax.fori_loop(0, X // 4, cstep, 0)

        def pstep(i, unused):
            lx, ly = i // (Y // 8), i % (Y // 8)
            ys = pl.ds(ly * 8, 8)

            def pair(ref):
                return jnp.concatenate([ref[2 * lx, ys, lanes], ref[2 * lx + 1, ys, lanes]], axis=1)

            c = pair(contrast)
            p = jnp.where(pair(cov) > 0, pair(pat), -1)
            phi, plo = p >> 4, p & 15
            vals = []
            power = c
            for q in range(3):
                high = power.astype(BF16).astype(F32)
                vals += [high, power - high]
                power = power * c
            lhs, rhs = [], []
            for s in range(8):
                def wide(v, n=8):
                    return jnp.broadcast_to(v[s:s + 1], (n, 2 * LANES))
                mask = wide(phi) == iota_hi
                parts = [jnp.where(mask, 1.0, 0.0)]
                parts += [jnp.where(mask, wide(v), 0.0) for v in vals]
                parts.append(jnp.zeros((8, 2 * LANES), F32))
                lhs.append(jnp.concatenate(parts, axis=0).astype(BF16))
                rhs.append(jnp.where(wide(plo, 16) == iota_lo, 1.0, 0.0).astype(BF16))
            acc[...] += lax.dot_general(
                jnp.concatenate(lhs, axis=1),
                jnp.concatenate(rhs, axis=1),
                (((1,), (1,)), ((), ())),
                preferred_element_type=F32,
            )
            return unused

        lax.fori_loop(0, X // 2 * (Y // 8), pstep, 0)

    for h in range(halves):
        @pl.when(me_r > 0)
        def _():
            xcopy(h, True).wait_recv()

        @pl.when(me_r < rows - 1)
        def _():
            xcopy(h, False).wait_recv()

        def xstep(t, unused):
            ys = pl.ds(t * 8, 8)
            both = jnp.concatenate(
                [xb[h, f, :, ys].reshape((X + 2 * W) * 8, LANES) for f in range(2)], axis=1
            )
            high, low = split(both)
            kh = kxhi[...]
            val = dot(kh, high) + dot(kxlo[...], high) + dot(kh, low)
            for f in range(2):
                yb[h, f, :, pl.ds(W + t * 8, 8)] = val[:, f * LANES:(f + 1) * LANES].reshape(X, 8, LANES)
            return unused

        lax.fori_loop(0, W // 8, xstep, 0)

        @pl.when(me_c > 0)
        def _():
            ycopy(h, False).start()

        lax.fori_loop(W // 8, Y // 8, xstep, 0)

        @pl.when(me_c < cols - 1)
        def _():
            ycopy(h, True).start()

        @pl.when(me_c > 0)
        def _():
            ycopy(h, True).wait_recv()

        @pl.when(me_c < cols - 1)
        def _():
            ycopy(h, False).wait_recv()

        finish(h)

    a = acc[...]
    terms = [a[0:8]] + [a[8 + 16 * q:16 + 16 * q] + a[16 + 16 * q:24 + 16 * q] for q in range(3)]
    spread = jnp.dot(
        jnp.concatenate(terms, axis=0), rep[...],
        precision=lax.Precision.HIGHEST, preferred_element_type=F32,
    )
    patch_hi = lax.broadcasted_iota(jnp.int32, (8, NPATCH), 1) // 16
    own = patch_hi == lax.broadcasted_iota(jnp.int32, (8, NPATCH), 0)
    for q in range(4):
        part = jnp.where(own, spread[8 * q:8 * q + 8], 0.0)
        srow[me_r, q:q + 1] = jnp.sum(part, axis=0, keepdims=True)
    srow[me_r, 4:8] = jnp.zeros((4, NPATCH), F32)
    scol[me_c] = add_up(gather_sum("row", rows, srow, s3, r3), srow, rows)
    whole = add_up(gather_sum("col", cols, scol, s4, r4), scol, cols)
    sums[...] = whole[0:4] * scale

    for h in range(halves):
        @pl.when(me_r > 0)
        def _():
            xcopy(h, False).wait_send()

        @pl.when(me_r < rows - 1)
        def _():
            xcopy(h, True).wait_send()

        @pl.when(me_c > 0)
        def _():
            ycopy(h, False).wait_send()

        @pl.when(me_c < cols - 1)
        def _():
            ycopy(h, True).wait_send()


def local(galaxy, randoms, coverage, patch):
    rows, cols = lax.axis_size("row"), lax.axis_size("col")
    X, Y, Z = galaxy.shape
    halves = Z // LANES
    W = RADIUS
    scale = NPATCH / (X * rows * Y * cols * Z)
    tz = split_np(band(Z, Z, 0).T)
    kx = split_np(np.kron(band(X, X + 2 * W, W), np.eye(8, dtype=np.float32)))
    ky = split_np(np.kron(np.eye(4, dtype=np.float32), band(Y, Y + 2 * W, W)))
    rep = (np.arange(NPATCH)[None, :] % 16 == np.arange(16)[:, None]).astype(np.float32)
    consts = [jnp.asarray(v) for v in (*tz, *kx, *ky, rep)]
    vmem = pl.BlockSpec(memory_space=pltpu.VMEM)
    dma = pltpu.SemaphoreType.DMA
    contrast, sums = pl.pallas_call(
        functools.partial(kernel, rows, cols, scale),
        out_shape=(
            jax.ShapeDtypeStruct((X, Y, Z), F32),
            jax.ShapeDtypeStruct((4, NPATCH), F32),
        ),
        in_specs=[vmem] * 11,
        out_specs=(vmem, vmem),
        scratch_shapes=[
            pltpu.VMEM((halves, 2, X + 2 * W, Y, LANES), F32),
            pltpu.VMEM((halves, 2, X, Y + 2 * W, LANES), F32),
            pltpu.VMEM((64, 16), F32),
            pltpu.VMEM((rows, 2, 8, LANES), F32),
            pltpu.VMEM((cols, 2, 8, LANES), F32),
            pltpu.VMEM((rows, 8, NPATCH), F32),
            pltpu.VMEM((cols, 8, NPATCH), F32),
            dma((halves, 2)), dma((halves, 2)), dma((halves, 2)), dma((halves, 2)),
            dma((rows - 1,)), dma((rows - 1,)), dma((cols - 1,)), dma((cols - 1,)),
            dma((rows - 1,)), dma((rows - 1,)), dma((cols - 1,)), dma((cols - 1,)),
        ],
        compiler_params=pltpu.CompilerParams(
            collective_id=0, has_side_effects=True, vmem_limit_bytes=40 * 1024 * 1024
        ),
    )(galaxy, randoms, coverage, patch, *consts)
    return contrast, sums


def solution(mesh):
    spec = P("row", "col", None)
    return jax.shard_map(
        local, mesh=mesh, in_specs=(spec,) * 4, out_specs=(spec, P()), check_vma=False
    )
```

```python
import functools

import jax
import jax.numpy as jnp
import ml_dtypes
import numpy as np
from jax import lax
from jax.experimental import pallas as pl
from jax.experimental.pallas import tpu as pltpu
from jax.sharding import PartitionSpec as P

RADIUS = 16
NPATCH = 128
LANES = 128
F32 = jnp.float32
BF16 = jnp.bfloat16
MESH = pl.DeviceIdType.MESH


def taps_np():
    offs = np.arange(-RADIUS, RADIUS + 1).astype(np.float32)
    sigma = RADIUS / 2.0
    vals = np.exp(-offs * offs / np.float32(2.0 * sigma * sigma)).astype(np.float32)
    return (vals / vals.sum(dtype=np.float32)).astype(np.float32)


def split_np(mat):
    high = mat.astype(ml_dtypes.bfloat16)
    low = (mat - high.astype(np.float32)).astype(ml_dtypes.bfloat16)
    return high, low


def band(outs, ins, shift):
    taps = taps_np()
    mat = np.zeros((outs, ins), np.float32)
    for o in range(outs):
        for j in range(-RADIUS, RADIUS + 1):
            i = o + j + shift
            if 0 <= i < ins:
                mat[o, i] = taps[j + RADIUS]
    return mat


def split(val):
    high = val.astype(BF16)
    low = (val - high.astype(F32)).astype(BF16)
    return high, low


def dot(a, b):
    return jnp.dot(a, b, preferred_element_type=F32)


def gather_sum(axis, size, buf, send, recv):
    me = lax.axis_index(axis)
    copies = []
    for k in range(1, size):
        copy = pltpu.make_async_remote_copy(
            src_ref=buf.at[me],
            dst_ref=buf.at[me],
            send_sem=send.at[k - 1],
            recv_sem=recv.at[k - 1],
            device_id={axis: lax.rem(me + k, size)},
            device_id_type=MESH,
        )
        copy.start()
        copies.append(copy)
    return copies


def add_up(copies, buf, size):
    for copy in copies:
        copy.wait()
    total = buf[0]
    for k in range(1, size):
        total = total + buf[k]
    return total


def kernel(
    rows, cols, scale,
    *refs,
):
    hbm, (contrast, sums), vmem = refs[:11], refs[11:13], refs[13:24]
    (
        xb, yb, acc, trow, tcol, srow, scol, sin,
        sx, rx, sy, ry, s1, r1, s2, r2, s3, r3, s4, r4,
    ) = refs[24:]
    gal, ran, cov, pat, thi, tlo, kxhi, kxlo, kyhi, kylo, rep = vmem
    X, Y, Z = gal.shape
    halves = Z // LANES
    W = RADIUS
    me_r = lax.axis_index("row")
    me_c = lax.axis_index("col")

    PX = 8
    slabs = X // PX
    def fetch(k, slab=None):
        at = slice(None) if slab is None else pl.ds(slab * PX, PX)
        return pltpu.make_async_copy(
            hbm[k].at[at], vmem[k].at[at], sin.at[k, 0 if slab is None else slab]
        )

    fetch(4).start()
    fetch(5).start()
    for i in range(slabs):
        fetch(0, i).start()
        fetch(1, i).start()
    for k in (6, 7, 2, 8, 9, 3, 10):
        fetch(k).start()

    barrier = pltpu.get_barrier_semaphore()
    for k in range(1, rows):
        pl.semaphore_signal(barrier, inc=1, device_id={"row": lax.rem(me_r + k, rows)}, device_id_type=MESH)
    for k in range(1, cols):
        pl.semaphore_signal(barrier, inc=1, device_id={"col": lax.rem(me_c + k, cols)}, device_id_type=MESH)
    fetch(4).wait()
    fetch(5).wait()

    def xcopy(h, up):
        own, far = ((X, 0) if up else (W, X + W))
        return pltpu.make_async_remote_copy(
            src_ref=xb.at[h, :, pl.ds(own, W)],
            dst_ref=xb.at[h, :, pl.ds(far, W)],
            send_sem=sx.at[h, int(up)],
            recv_sem=rx.at[h, int(up)],
            device_id={"row": lax.rem(me_r + (1 if up else rows - 1), rows)},
            device_id_type=MESH,
        )

    def ycopy(h, up):
        own, far = ((Y, 0) if up else (W, Y + W))
        return pltpu.make_async_remote_copy(
            src_ref=yb.at[h, :, :, pl.ds(own, W)],
            dst_ref=yb.at[h, :, :, pl.ds(far, W)],
            send_sem=sy.at[h, int(up)],
            recv_sem=ry.at[h, int(up)],
            device_id={"col": lax.rem(me_c + (1 if up else cols - 1), cols)},
            device_id_type=MESH,
        )

    def xstart(h):
        @pl.when(me_r > 0)
        def _():
            xcopy(h, False).start()

        @pl.when(me_r < rows - 1)
        def _():
            xcopy(h, True).start()

    def xsent(h):
        @pl.when(me_r > 0)
        def _():
            xcopy(h, False).wait_send()

        @pl.when(me_r < rows - 1)
        def _():
            xcopy(h, True).wait_send()

    for h in range(halves):
        lanes = pl.ds(h * LANES, LANES)

        def zstep(i, unused):
            for f, ref in enumerate((gal, ran)):
                high, low = split(ref[pl.ds(i * PX, PX)].reshape(PX * Y, Z))
                th = thi[:, lanes]
                val = dot(high, th) + dot(high, tlo[:, lanes]) + dot(low, th)
                xb[h, f, pl.ds(W + i * PX, PX)] = val.reshape(PX, Y, LANES)
            return unused

        for i in range(slabs):
            if h == 0:
                fetch(0, i).wait()
                fetch(1, i).wait()
            zstep(i, 0)
        if h == 0:
            pl.semaphore_wait(barrier, rows + cols - 2)
            xstart(h)

        @pl.when(me_r == 0)
        def _():
            xb[h, :, 0:W] = jnp.zeros((2, W, Y, LANES), F32)

        @pl.when(me_r == rows - 1)
        def _():
            xb[h, :, X + W:] = jnp.zeros((2, W, Y, LANES), F32)

        @pl.when(me_c == 0)
        def _():
            yb[h, :, :, 0:W] = jnp.zeros((2, X, W, LANES), F32)

        @pl.when(me_c == cols - 1)
        def _():
            yb[h, :, :, Y + W:] = jnp.zeros((2, X, W, LANES), F32)

    for k in (2, 3, 6, 7, 8, 9, 10):
        fetch(k).wait()

    def tstep(i, carry):
        m = cov[i].astype(F32)
        g = (m * gal[i]).reshape(Y // 8, 8, Z).sum(axis=0)
        r = (m * ran[i]).reshape(Y // 8, 8, Z).sum(axis=0)
        return carry[0] + g, carry[1] + r

    zero = jnp.zeros((8, Z), F32)
    tg, tr = lax.fori_loop(0, X, tstep, (zero, zero))
    for f, t in enumerate((tg, tr)):
        trow[me_r, f] = sum(t[:, k * LANES:(k + 1) * LANES] for k in range(Z // LANES))
    tcol[me_c] = add_up(gather_sum("row", rows, trow, s1, r1), trow, rows)
    tot = add_up(gather_sum("col", cols, tcol, s2, r2), tcol, cols)
    alpha = jnp.sum(tot[0], keepdims=True) / jnp.sum(tot[1], keepdims=True)

    acc[...] = jnp.zeros_like(acc)
    iota_hi = lax.broadcasted_iota(jnp.int32, (8, 2 * LANES), 0)
    iota_lo = lax.broadcasted_iota(jnp.int32, (16, 2 * LANES), 0)

    def finish(h):
        lanes = pl.ds(h * LANES, LANES)

        def cstep(i, unused):
            x4 = pl.ds(i * 4, 4)
            both = jnp.concatenate(
                [yb[h, f, x4].reshape(4 * (Y + 2 * W), LANES) for f in range(2)], axis=1
            )
            high, low = split(both)
            kh = kyhi[...]
            val = dot(kh, high) + dot(kylo[...], high) + dot(kh, low)
            m = cov[x4, :, lanes].astype(F32).reshape(4 * Y, LANES)
            nbar = alpha * val[:, LANES:]
            weight = 1.0 / (1.0 + 2.0 * nbar)
            c = m * weight * (val[:, :LANES] / nbar - 1.0)
            contrast[x4, :, lanes] = c.reshape(4, Y, LANES)
            return unused

        lax.fori_loop(0, X // 4, cstep, 0)

        def pstep(i, unused):
            lx, ly = i // (Y // 8), i % (Y // 8)
            ys = pl.ds(ly * 8, 8)

            def pair(ref):
                return jnp.concatenate([ref[2 * lx, ys, lanes], ref[2 * lx + 1, ys, lanes]], axis=1)

            c = pair(contrast)
            p = jnp.where(pair(cov) > 0, pair(pat), -1)
            phi, plo = p >> 4, p & 15
            vals = []
            power = c
            for q in range(3):
                high = power.astype(BF16).astype(F32)
                vals += [high, power - high]
                power = power * c
            lhs, rhs = [], []
            for s in range(8):
                def wide(v, n=8):
                    return jnp.broadcast_to(v[s:s + 1], (n, 2 * LANES))
                mask = wide(phi) == iota_hi
                parts = [jnp.where(mask, 1.0, 0.0)]
                parts += [jnp.where(mask, wide(v), 0.0) for v in vals]
                parts.append(jnp.zeros((8, 2 * LANES), F32))
                lhs.append(jnp.concatenate(parts, axis=0).astype(BF16))
                rhs.append(jnp.where(wide(plo, 16) == iota_lo, 1.0, 0.0).astype(BF16))
            acc[...] += lax.dot_general(
                jnp.concatenate(lhs, axis=1),
                jnp.concatenate(rhs, axis=1),
                (((1,), (1,)), ((), ())),
                preferred_element_type=F32,
            )
            return unused

        lax.fori_loop(0, X // 2 * (Y // 8), pstep, 0)

    for h in range(halves):
        @pl.when(me_r > 0)
        def _():
            xcopy(h, True).wait_recv()

        @pl.when(me_r < rows - 1)
        def _():
            xcopy(h, False).wait_recv()

        xsent(h)
        if h + 1 < halves:
            xstart(h + 1)

        def xstep(t, unused):
            ys = pl.ds(t * 8, 8)
            both = jnp.concatenate(
                [xb[h, f, :, ys].reshape((X + 2 * W) * 8, LANES) for f in range(2)], axis=1
            )
            high, low = split(both)
            kh = kxhi[...]
            val = dot(kh, high) + dot(kxlo[...], high) + dot(kh, low)
            for f in range(2):
                yb[h, f, :, pl.ds(W + t * 8, 8)] = val[:, f * LANES:(f + 1) * LANES].reshape(X, 8, LANES)
            return unused

        lax.fori_loop(0, W // 8, xstep, 0)

        @pl.when(me_c > 0)
        def _():
            ycopy(h, False).start()

        lax.fori_loop(W // 8, Y // 8, xstep, 0)

        @pl.when(me_c < cols - 1)
        def _():
            ycopy(h, True).start()

        @pl.when(me_c > 0)
        def _():
            ycopy(h, True).wait_recv()

        @pl.when(me_c < cols - 1)
        def _():
            ycopy(h, False).wait_recv()

        finish(h)

    a = acc[...]
    terms = [a[0:8]] + [a[8 + 16 * q:16 + 16 * q] + a[16 + 16 * q:24 + 16 * q] for q in range(3)]
    spread = jnp.dot(
        jnp.concatenate(terms, axis=0), rep[...],
        precision=lax.Precision.HIGHEST, preferred_element_type=F32,
    )
    patch_hi = lax.broadcasted_iota(jnp.int32, (8, NPATCH), 1) // 16
    own = patch_hi == lax.broadcasted_iota(jnp.int32, (8, NPATCH), 0)
    for q in range(4):
        part = jnp.where(own, spread[8 * q:8 * q + 8], 0.0)
        srow[me_r, q:q + 1] = jnp.sum(part, axis=0, keepdims=True)
    srow[me_r, 4:8] = jnp.zeros((4, NPATCH), F32)
    scol[me_c] = add_up(gather_sum("row", rows, srow, s3, r3), srow, rows)
    whole = add_up(gather_sum("col", cols, scol, s4, r4), scol, cols)
    sums[...] = whole[0:4] * scale

    for h in range(halves):
        @pl.when(me_c > 0)
        def _():
            ycopy(h, False).wait_send()

        @pl.when(me_c < cols - 1)
        def _():
            ycopy(h, True).wait_send()


def local(galaxy, randoms, coverage, patch):
    rows, cols = lax.axis_size("row"), lax.axis_size("col")
    X, Y, Z = galaxy.shape
    halves = Z // LANES
    W = RADIUS
    scale = NPATCH / (X * rows * Y * cols * Z)
    tz = split_np(band(Z, Z, 0).T)
    kx = split_np(np.kron(band(X, X + 2 * W, W), np.eye(8, dtype=np.float32)))
    ky = split_np(np.kron(np.eye(4, dtype=np.float32), band(Y, Y + 2 * W, W)))
    rep = (np.arange(NPATCH)[None, :] % 16 == np.arange(16)[:, None]).astype(np.float32)
    consts = [jnp.asarray(v) for v in (*tz, *kx, *ky, rep)]
    args = (galaxy, randoms, coverage, patch, *consts)
    vmem = pl.BlockSpec(memory_space=pltpu.VMEM)
    dma = pltpu.SemaphoreType.DMA
    contrast, sums = pl.pallas_call(
        functools.partial(kernel, rows, cols, scale),
        out_shape=(
            jax.ShapeDtypeStruct((X, Y, Z), F32),
            jax.ShapeDtypeStruct((4, NPATCH), F32),
        ),
        in_specs=[pl.BlockSpec(memory_space=pl.ANY)] * 11,
        out_specs=(vmem, vmem),
        scratch_shapes=[pltpu.VMEM(v.shape, v.dtype) for v in args] + [
            pltpu.VMEM((halves, 2, X + 2 * W, Y, LANES), F32),
            pltpu.VMEM((halves, 2, X, Y + 2 * W, LANES), F32),
            pltpu.VMEM((64, 16), F32),
            pltpu.VMEM((rows, 2, 8, LANES), F32),
            pltpu.VMEM((cols, 2, 8, LANES), F32),
            pltpu.VMEM((rows, 8, NPATCH), F32),
            pltpu.VMEM((cols, 8, NPATCH), F32),
            dma((11, X // 8)),
            dma((halves, 2)), dma((halves, 2)), dma((halves, 2)), dma((halves, 2)),
            dma((rows - 1,)), dma((rows - 1,)), dma((cols - 1,)), dma((cols - 1,)),
            dma((rows - 1,)), dma((rows - 1,)), dma((cols - 1,)), dma((cols - 1,)),
        ],
        compiler_params=pltpu.CompilerParams(
            collective_id=0, has_side_effects=True, vmem_limit_bytes=60 * 1024 * 1024
        ),
    )(*args)
    return contrast, sums


def solution(mesh):
    spec = P("row", "col", None)
    return jax.shard_map(
        local, mesh=mesh, in_specs=(spec,) * 4, out_specs=(spec, P()), check_vma=False
    )
```

```python
import functools

import jax
import jax.numpy as jnp
import ml_dtypes
import numpy as np
from jax import lax
from jax.experimental import pallas as pl
from jax.experimental.pallas import tpu as pltpu
from jax.sharding import PartitionSpec as P

RADIUS = 16
NPATCH = 128
LANES = 128
F32 = jnp.float32
BF16 = jnp.bfloat16
MESH = pl.DeviceIdType.MESH


def taps_np():
    offs = np.arange(-RADIUS, RADIUS + 1).astype(np.float32)
    sigma = RADIUS / 2.0
    vals = np.exp(-offs * offs / np.float32(2.0 * sigma * sigma)).astype(np.float32)
    return (vals / vals.sum(dtype=np.float32)).astype(np.float32)


def split_np(mat):
    high = mat.astype(ml_dtypes.bfloat16)
    low = (mat - high.astype(np.float32)).astype(ml_dtypes.bfloat16)
    return high, low


def band(outs, ins, shift):
    taps = taps_np()
    mat = np.zeros((outs, ins), np.float32)
    for o in range(outs):
        for j in range(-RADIUS, RADIUS + 1):
            i = o + j + shift
            if 0 <= i < ins:
                mat[o, i] = taps[j + RADIUS]
    return mat


def split(val):
    high = val.astype(BF16)
    low = (val - high.astype(F32)).astype(BF16)
    return high, low


def dot(a, b):
    return jnp.dot(a, b, preferred_element_type=F32)


def gather_sum(axis, size, buf, send, recv):
    me = lax.axis_index(axis)
    copies = []
    for k in range(1, size):
        copy = pltpu.make_async_remote_copy(
            src_ref=buf.at[me],
            dst_ref=buf.at[me],
            send_sem=send.at[k - 1],
            recv_sem=recv.at[k - 1],
            device_id={axis: lax.rem(me + k, size)},
            device_id_type=MESH,
        )
        copy.start()
        copies.append(copy)
    return copies


def add_up(copies, buf, size):
    for copy in copies:
        copy.wait()
    total = buf[0]
    for k in range(1, size):
        total = total + buf[k]
    return total


def kernel(
    rows, cols, scale,
    *refs,
):
    hbm, (contrast, sums), vmem = refs[:11], refs[11:13], refs[13:24]
    (
        xb, yb, acc, trow, tcol, srow, scol, rb, oh, rh, sin,
        sx, rx, sy, ry, srel, rrel, s1, r1, s2, r2, s3, r3, s4, r4,
    ) = refs[24:]
    gal, ran, cov, pat, thi, tlo, kxhi, kxlo, kyhi, kylo, rep = vmem
    X, Y, Z = gal.shape
    halves = Z // LANES
    W = RADIUS
    me_r = lax.axis_index("row")
    me_c = lax.axis_index("col")

    PX = 8
    slabs = X // PX
    def fetch(k, slab=None):
        at = slice(None) if slab is None else pl.ds(slab * PX, PX)
        return pltpu.make_async_copy(
            hbm[k].at[at], vmem[k].at[at], sin.at[k, 0 if slab is None else slab]
        )

    fetch(4).start()
    fetch(5).start()
    for i in range(slabs):
        fetch(0, i).start()
        fetch(1, i).start()
    for k in (6, 7, 2, 8, 9, 3, 10):
        fetch(k).start()

    barrier = pltpu.get_barrier_semaphore()
    for k in range(1, rows):
        pl.semaphore_signal(barrier, inc=1, device_id={"row": lax.rem(me_r + k, rows)}, device_id_type=MESH)
    for k in range(1, cols):
        pl.semaphore_signal(barrier, inc=1, device_id={"col": lax.rem(me_c + k, cols)}, device_id_type=MESH)
    fetch(4).wait()
    fetch(5).wait()

    relayed = rows == 4
    YP = Y // 2

    def xsrc(h, up, part):
        return xb.at[h, :, pl.ds(X if up else W, W), pl.ds(part * YP, YP)]

    def xdst(h, up, part):
        return xb.at[h, :, pl.ds(0 if up else X + W, W), pl.ds(part * YP, YP)]

    def xsend(src, dst, ssem, rsem, hop):
        return pltpu.make_async_remote_copy(
            src_ref=src, dst_ref=dst, send_sem=ssem, recv_sem=rsem,
            device_id={"row": lax.rem(me_r + (hop + rows), rows)}, device_id_type=MESH,
        )

    def xcopy(h, up, part):
        u = int(up)
        return xsend(xsrc(h, up, part), xdst(h, up, part), sx.at[h, u, part], rx.at[h, u, part], 1 if up else -1)

    def xfirst(h, up):
        return xsend(xsrc(h, up, 1), rb.at[h], sx.at[h, int(up), 1], rrel.at[h], 2 if up else -2)

    def xsecond(h, up):
        return xsend(rb.at[h], xdst(h, up, 1), srel.at[h], rx.at[h, int(up), 1], -1 if up else 1)

    def xeach(h, act):
        for part in (1, 0):
            for up in (False, True):
                has = me_r < rows - 1 if up else me_r > 0
                if relayed and part == 1:
                    turn = me_r == (1 if up else 2)

                    @pl.when(turn)
                    def _():
                        act(xfirst(h, up))

                    has = jnp.logical_and(has, jnp.logical_not(turn))

                @pl.when(has)
                def _():
                    act(xcopy(h, up, part))

    def relay(h, act):
        if relayed:
            for up in (False, True):
                @pl.when(me_r == (3 if up else 0))
                def _():
                    act(xsecond(h, up))

    def relay_on(h):
        if relayed:
            for up in (False, True):
                @pl.when(me_r == (3 if up else 0))
                def _():
                    xfirst(h, up).wait_recv()
                    xsecond(h, up).start()

    def xarrived(h, part):
        @pl.when(me_r > 0)
        def _():
            xcopy(h, True, part).wait_recv()

        @pl.when(me_r < rows - 1)
        def _():
            xcopy(h, False, part).wait_recv()

    def ycopy(h, up):
        own, far = ((Y, 0) if up else (W, Y + W))
        return pltpu.make_async_remote_copy(
            src_ref=yb.at[h, :, :, pl.ds(own, W)],
            dst_ref=yb.at[h, :, :, pl.ds(far, W)],
            send_sem=sy.at[h, int(up)],
            recv_sem=ry.at[h, int(up)],
            device_id={"col": lax.rem(me_c + (1 if up else cols - 1), cols)},
            device_id_type=MESH,
        )

    def xstart(h):
        xeach(h, lambda copy: copy.start())

    def xsent(h):
        xeach(h, lambda copy: copy.wait_send())

    for h in range(halves):
        lanes = pl.ds(h * LANES, LANES)

        def zstep(i, unused):
            for f, ref in enumerate((gal, ran)):
                high, low = split(ref[pl.ds(i * PX, PX)].reshape(PX * Y, Z))
                th = thi[:, lanes]
                val = dot(high, th) + dot(high, tlo[:, lanes]) + dot(low, th)
                xb[h, f, pl.ds(W + i * PX, PX)] = val.reshape(PX, Y, LANES)
            return unused

        for i in range(slabs):
            if h == 0:
                fetch(0, i).wait()
                fetch(1, i).wait()
            zstep(i, 0)
        if h == 0:
            pl.semaphore_wait(barrier, rows + cols - 2)
            xstart(h)

        @pl.when(me_r == 0)
        def _():
            xb[h, :, 0:W] = jnp.zeros((2, W, Y, LANES), F32)

        @pl.when(me_r == rows - 1)
        def _():
            xb[h, :, X + W:] = jnp.zeros((2, W, Y, LANES), F32)

        @pl.when(me_c == 0)
        def _():
            yb[h, :, :, 0:W] = jnp.zeros((2, X, W, LANES), F32)

        @pl.when(me_c == cols - 1)
        def _():
            yb[h, :, :, Y + W:] = jnp.zeros((2, X, W, LANES), F32)

    for k in (2, 3, 6, 7, 8, 9, 10):
        fetch(k).wait()

    def tstep(i, carry):
        m = cov[i].astype(F32)
        g = (m * gal[i]).reshape(Y // 8, 8, Z).sum(axis=0)
        r = (m * ran[i]).reshape(Y // 8, 8, Z).sum(axis=0)
        return carry[0] + g, carry[1] + r

    zero = jnp.zeros((8, Z), F32)
    tg, tr = lax.fori_loop(0, X, tstep, (zero, zero))
    for f, t in enumerate((tg, tr)):
        trow[me_r, f] = sum(t[:, k * LANES:(k + 1) * LANES] for k in range(Z // LANES))
    row_totals = gather_sum("row", rows, trow, s1, r1)

    acc[...] = jnp.zeros_like(acc)
    iota = lax.broadcasted_iota(jnp.int32, (8, 2 * LANES), 0)

    def pair(ref, h, i):
        lx, ys, lanes = i // (Y // 8), pl.ds(i % (Y // 8) * 8, 8), pl.ds(h * LANES, LANES)
        return jnp.concatenate([ref[2 * lx, ys, lanes], ref[2 * lx + 1, ys, lanes]], axis=1)

    def wide(v, s):
        return jnp.broadcast_to(v[s:s + 1], (8, 2 * LANES))

    def onehots(h):
        def step(i, unused):
            p = jnp.where(pair(cov, h, i) > 0, pair(pat, h, i), -1)
            phi, plo = p >> 4, p & 15
            for s in range(8):
                at = pl.ds(s * 2 * LANES, 2 * LANES)
                one = jnp.where(wide(phi, s) == iota, 1.0, 0.0)
                oh[h, i, :, at] = jnp.concatenate([one, one], axis=0).astype(BF16)
                lows = [jnp.where(wide(plo, s) == iota + k, 1.0, 0.0) for k in (0, 8)]
                rh[h, i, :, at] = jnp.concatenate(lows, axis=0).astype(BF16)
            return unused

        lax.fori_loop(0, X // 2 * (Y // 8), step, 0)

    def finish(h, alpha):
        lanes = pl.ds(h * LANES, LANES)

        def cstep(i, unused):
            x4 = pl.ds(i * 4, 4)
            both = jnp.concatenate(
                [yb[h, f, x4].reshape(4 * (Y + 2 * W), LANES) for f in range(2)], axis=1
            )
            high, low = split(both)
            kh = kyhi[...]
            val = dot(kh, high) + dot(kylo[...], high) + dot(kh, low)
            m = cov[x4, :, lanes].astype(F32).reshape(4 * Y, LANES)
            nbar = alpha * val[:, LANES:]
            weight = 1.0 / (1.0 + 2.0 * nbar)
            c = m * weight * (val[:, :LANES] / nbar - 1.0)
            contrast[x4, :, lanes] = c.reshape(4, Y, LANES)
            return unused

        lax.fori_loop(0, X // 4, cstep, 0)

        def pstep(i, unused):
            c = pair(contrast, h, i)
            terms = [oh[h, i]]
            power = c
            for q in range(3):
                high, low = split(power)
                high, low = high.astype(F32), low.astype(F32)
                terms.append(jnp.concatenate([
                    jnp.concatenate([wide(high, s), wide(low, s)], axis=0).astype(BF16)
                    for s in range(8)
                ], axis=1) * oh[h, i])
                power = power * c
            acc[...] += lax.dot_general(
                rh[h, i], jnp.concatenate(terms, axis=0), (((1,), (1,)), ((), ())),
                preferred_element_type=F32,
            )
            return unused

        lax.fori_loop(0, X // 2 * (Y // 8), pstep, 0)

    for h in range(halves):
        def xstep(t, unused):
            ys = pl.ds(t * 8, 8)
            both = jnp.concatenate(
                [xb[h, f, :, ys].reshape((X + 2 * W) * 8, LANES) for f in range(2)], axis=1
            )
            high, low = split(both)
            kh = kxhi[...]
            val = dot(kh, high) + dot(kxlo[...], high) + dot(kh, low)
            for f in range(2):
                yb[h, f, :, pl.ds(W + t * 8, 8)] = val[:, f * LANES:(f + 1) * LANES].reshape(X, 8, LANES)
            return unused

        if h == 0:
            relay_on(0)
            onehots(0)
        xarrived(h, 0)
        if h == 0:
            tcol[me_c] = add_up(row_totals, trow, rows)
            col_totals = gather_sum("col", cols, tcol, s2, r2)
        lax.fori_loop(0, W // 8, xstep, 0)

        @pl.when(me_c > 0)
        def _():
            ycopy(h, False).start()

        xarrived(h, 1)
        xsent(h)
        if h + 1 < halves:
            xstart(h + 1)
        lax.fori_loop(W // 8, Y // 8, xstep, 0)

        @pl.when(me_c < cols - 1)
        def _():
            ycopy(h, True).start()

        if h > 0:
            onehots(h)

        @pl.when(me_c > 0)
        def _():
            ycopy(h, True).wait_recv()

        @pl.when(me_c < cols - 1)
        def _():
            ycopy(h, False).wait_recv()

        if h + 1 < halves:
            relay_on(h + 1)
        if h == 0:
            tot = add_up(col_totals, tcol, cols)
            alpha = jnp.sum(tot[0], keepdims=True) / jnp.sum(tot[1], keepdims=True)
        finish(h, alpha)

    a = acc[...].T
    terms = [a[0:8]] + [a[16 * q:16 * q + 8] + a[16 * q + 8:16 * q + 16] for q in range(1, 4)]
    spread = jnp.dot(
        jnp.concatenate(terms, axis=0), rep[...],
        precision=lax.Precision.HIGHEST, preferred_element_type=F32,
    )
    patch_hi = lax.broadcasted_iota(jnp.int32, (8, NPATCH), 1) // 16
    own = patch_hi == lax.broadcasted_iota(jnp.int32, (8, NPATCH), 0)
    for q in range(4):
        part = jnp.where(own, spread[8 * q:8 * q + 8], 0.0)
        srow[me_r, q:q + 1] = jnp.sum(part, axis=0, keepdims=True)
    srow[me_r, 4:8] = jnp.zeros((4, NPATCH), F32)
    scol[me_c] = add_up(gather_sum("row", rows, srow, s3, r3), srow, rows)
    whole = add_up(gather_sum("col", cols, scol, s4, r4), scol, cols)
    sums[...] = whole[0:4] * scale

    for h in range(halves):
        relay(h, lambda copy: copy.wait_send())

        @pl.when(me_c > 0)
        def _():
            ycopy(h, False).wait_send()

        @pl.when(me_c < cols - 1)
        def _():
            ycopy(h, True).wait_send()


def local(galaxy, randoms, coverage, patch):
    rows, cols = lax.axis_size("row"), lax.axis_size("col")
    X, Y, Z = galaxy.shape
    halves = Z // LANES
    W = RADIUS
    scale = NPATCH / (X * rows * Y * cols * Z)
    tz = split_np(band(Z, Z, 0).T)
    kx = split_np(np.kron(band(X, X + 2 * W, W), np.eye(8, dtype=np.float32)))
    ky = split_np(np.kron(np.eye(4, dtype=np.float32), band(Y, Y + 2 * W, W)))
    rep = (np.arange(NPATCH)[None, :] % 16 == np.arange(16)[:, None]).astype(np.float32)
    consts = [jnp.asarray(v) for v in (*tz, *kx, *ky, rep)]
    args = (galaxy, randoms, coverage, patch, *consts)
    vmem = pl.BlockSpec(memory_space=pltpu.VMEM)
    dma = pltpu.SemaphoreType.DMA
    contrast, sums = pl.pallas_call(
        functools.partial(kernel, rows, cols, scale),
        out_shape=(
            jax.ShapeDtypeStruct((X, Y, Z), F32),
            jax.ShapeDtypeStruct((4, NPATCH), F32),
        ),
        in_specs=[pl.BlockSpec(memory_space=pl.ANY)] * 11,
        out_specs=(vmem, vmem),
        scratch_shapes=[pltpu.VMEM(v.shape, v.dtype) for v in args] + [
            pltpu.VMEM((halves, 2, X + 2 * W, Y, LANES), F32),
            pltpu.VMEM((halves, 2, X, Y + 2 * W, LANES), F32),
            pltpu.VMEM((16, 64), F32),
            pltpu.VMEM((rows, 2, 8, LANES), F32),
            pltpu.VMEM((cols, 2, 8, LANES), F32),
            pltpu.VMEM((rows, 8, NPATCH), F32),
            pltpu.VMEM((cols, 8, NPATCH), F32),
            pltpu.VMEM((halves, 2, W, Y // 2, LANES), F32),
            pltpu.VMEM((halves, X // 2 * (Y // 8), 16, 16 * LANES), BF16),
            pltpu.VMEM((halves, X // 2 * (Y // 8), 16, 16 * LANES), BF16),
            dma((11, X // 8)),
            dma((halves, 2, 2)), dma((halves, 2, 2)), dma((halves, 2)), dma((halves, 2)),
            dma((halves,)), dma((halves,)),
            dma((rows - 1,)), dma((rows - 1,)), dma((cols - 1,)), dma((cols - 1,)),
            dma((rows - 1,)), dma((rows - 1,)), dma((cols - 1,)), dma((cols - 1,)),
        ],
        compiler_params=pltpu.CompilerParams(
            collective_id=0, has_side_effects=True, vmem_limit_bytes=60 * 1024 * 1024
        ),
    )(*args)
    return contrast, sums


def solution(mesh):
    spec = P("row", "col", None)
    return jax.shard_map(
        local, mesh=mesh, in_specs=(spec,) * 4, out_specs=(spec, P()), check_vma=False
    )
```

```python
import functools

import jax
import jax.numpy as jnp
import ml_dtypes
import numpy as np
from jax import lax
from jax.experimental import pallas as pl
from jax.experimental.pallas import tpu as pltpu
from jax.sharding import PartitionSpec as P

RADIUS = 16
NPATCH = 128
LANES = 128
F32 = jnp.float32
BF16 = jnp.bfloat16
MESH = pl.DeviceIdType.MESH


def taps_np():
    offs = np.arange(-RADIUS, RADIUS + 1).astype(np.float32)
    sigma = RADIUS / 2.0
    vals = np.exp(-offs * offs / np.float32(2.0 * sigma * sigma)).astype(np.float32)
    return (vals / vals.sum(dtype=np.float32)).astype(np.float32)


def split_np(mat):
    high = mat.astype(ml_dtypes.bfloat16)
    low = (mat - high.astype(np.float32)).astype(ml_dtypes.bfloat16)
    return high, low


def band(outs, ins, shift):
    taps = taps_np()
    mat = np.zeros((outs, ins), np.float32)
    for o in range(outs):
        for j in range(-RADIUS, RADIUS + 1):
            i = o + j + shift
            if 0 <= i < ins:
                mat[o, i] = taps[j + RADIUS]
    return mat


def split(val):
    high = val.astype(BF16)
    low = (val - high.astype(F32)).astype(BF16)
    return high, low


def dot(a, b):
    return jnp.dot(a, b, preferred_element_type=F32)


def gather_sum(axis, size, buf, send, recv):
    me = lax.axis_index(axis)
    copies = []
    for k in range(1, size):
        copy = pltpu.make_async_remote_copy(
            src_ref=buf.at[me],
            dst_ref=buf.at[me],
            send_sem=send.at[k - 1],
            recv_sem=recv.at[k - 1],
            device_id={axis: lax.rem(me + k, size)},
            device_id_type=MESH,
        )
        copy.start()
        copies.append(copy)
    return copies


def add_up(copies, buf, size):
    for copy in copies:
        copy.wait()
    total = buf[0]
    for k in range(1, size):
        total = total + buf[k]
    return total


def kernel(
    rows, cols, scale,
    *refs,
):
    hbm, (contrast, sums), vmem = refs[:11], refs[11:13], refs[13:24]
    (
        xb, yb, acc, trow, tcol, srow, scol, rb, oh, rh, sin,
        sx, rx, sy, ry, srel, rrel, s1, r1, s2, r2, s3, r3, s4, r4,
    ) = refs[24:]
    gal, ran, cov, pat, thi, tlo, kxhi, kxlo, kyhi, kylo, rep = vmem
    X, Y, Z = gal.shape
    halves = Z // LANES
    W = RADIUS
    me_r = lax.axis_index("row")
    me_c = lax.axis_index("col")

    PX = 8
    slabs = X // PX
    def fetch(k, slab=None):
        at = slice(None) if slab is None else pl.ds(slab * PX, PX)
        return pltpu.make_async_copy(
            hbm[k].at[at], vmem[k].at[at], sin.at[k, 0 if slab is None else slab]
        )

    fetch(4).start()
    fetch(5).start()
    for i in range(slabs):
        fetch(0, i).start()
        fetch(1, i).start()
    for k in (6, 7, 2, 8, 9, 3, 10):
        fetch(k).start()

    barrier = pltpu.get_barrier_semaphore()
    for k in range(1, rows):
        pl.semaphore_signal(barrier, inc=1, device_id={"row": lax.rem(me_r + k, rows)}, device_id_type=MESH)
    for k in range(1, cols):
        pl.semaphore_signal(barrier, inc=1, device_id={"col": lax.rem(me_c + k, cols)}, device_id_type=MESH)
    fetch(4).wait()
    fetch(5).wait()

    relayed = rows == 4
    YP = Y // 2

    def xsrc(h, up, part):
        return xb.at[h, :, pl.ds(X if up else W, W), pl.ds(part * YP, YP)]

    def xdst(h, up, part):
        return xb.at[h, :, pl.ds(0 if up else X + W, W), pl.ds(part * YP, YP)]

    def xsend(src, dst, ssem, rsem, hop):
        return pltpu.make_async_remote_copy(
            src_ref=src, dst_ref=dst, send_sem=ssem, recv_sem=rsem,
            device_id={"row": lax.rem(me_r + (hop + rows), rows)}, device_id_type=MESH,
        )

    def xcopy(h, up, part):
        u = int(up)
        return xsend(xsrc(h, up, part), xdst(h, up, part), sx.at[h, u, part], rx.at[h, u, part], 1 if up else -1)

    def xfirst(h, up):
        return xsend(xsrc(h, up, 1), rb.at[h], sx.at[h, int(up), 1], rrel.at[h], 2 if up else -2)

    def xsecond(h, up):
        return xsend(rb.at[h], xdst(h, up, 1), srel.at[h], rx.at[h, int(up), 1], -1 if up else 1)

    def xeach(h, act):
        for part in (1, 0):
            for up in (False, True):
                has = me_r < rows - 1 if up else me_r > 0
                if relayed and part == 1:
                    turn = me_r == (1 if up else 2)

                    @pl.when(turn)
                    def _():
                        act(xfirst(h, up))

                    has = jnp.logical_and(has, jnp.logical_not(turn))

                @pl.when(has)
                def _():
                    act(xcopy(h, up, part))

    def relay(h, act):
        if relayed:
            for up in (False, True):
                @pl.when(me_r == (3 if up else 0))
                def _():
                    act(xsecond(h, up))

    def relay_on(h):
        if relayed:
            for up in (False, True):
                @pl.when(me_r == (3 if up else 0))
                def _():
                    xfirst(h, up).wait_recv()
                    xsecond(h, up).start()

    def xarrived(h, part):
        @pl.when(me_r > 0)
        def _():
            xcopy(h, True, part).wait_recv()

        @pl.when(me_r < rows - 1)
        def _():
            xcopy(h, False, part).wait_recv()

    def ycopy(h, up):
        own, far = ((Y, 0) if up else (W, Y + W))
        return pltpu.make_async_remote_copy(
            src_ref=yb.at[h, :, :, pl.ds(own, W)],
            dst_ref=yb.at[h, :, :, pl.ds(far, W)],
            send_sem=sy.at[h, int(up)],
            recv_sem=ry.at[h, int(up)],
            device_id={"col": lax.rem(me_c + (1 if up else cols - 1), cols)},
            device_id_type=MESH,
        )

    def xstart(h):
        xeach(h, lambda copy: copy.start())

    def xsent(h):
        xeach(h, lambda copy: copy.wait_send())

    for h in range(halves):
        lanes = pl.ds(h * LANES, LANES)

        def zstep(i, unused):
            for f, ref in enumerate((gal, ran)):
                high, low = split(ref[pl.ds(i * PX, PX)].reshape(PX * Y, Z))
                th = thi[:, lanes]
                val = dot(high, th) + dot(high, tlo[:, lanes]) + dot(low, th)
                xb[h, f, pl.ds(W + i * PX, PX)] = val.reshape(PX, Y, LANES)
            return unused

        for i in range(slabs):
            if h == 0:
                fetch(0, i).wait()
                fetch(1, i).wait()
            zstep(i, 0)
        if h == 0:
            pl.semaphore_wait(barrier, rows + cols - 2)
            xstart(h)

        @pl.when(me_r == 0)
        def _():
            xb[h, :, 0:W] = jnp.zeros((2, W, Y, LANES), F32)

        @pl.when(me_r == rows - 1)
        def _():
            xb[h, :, X + W:] = jnp.zeros((2, W, Y, LANES), F32)

        @pl.when(me_c == 0)
        def _():
            yb[h, :, :, 0:W] = jnp.zeros((2, X, W, LANES), F32)

        @pl.when(me_c == cols - 1)
        def _():
            yb[h, :, :, Y + W:] = jnp.zeros((2, X, W, LANES), F32)

    for k in (2, 3, 6, 7, 8, 9, 10):
        fetch(k).wait()

    def tstep(i, carry):
        m = cov[i].astype(F32)
        g = (m * gal[i]).reshape(Y // 8, 8, Z).sum(axis=0)
        r = (m * ran[i]).reshape(Y // 8, 8, Z).sum(axis=0)
        return carry[0] + g, carry[1] + r

    zero = jnp.zeros((8, Z), F32)
    tg, tr = lax.fori_loop(0, X, tstep, (zero, zero))
    for f, t in enumerate((tg, tr)):
        trow[me_r, f] = sum(t[:, k * LANES:(k + 1) * LANES] for k in range(Z // LANES))
    row_totals = gather_sum("row", rows, trow, s1, r1)

    acc[...] = jnp.zeros_like(acc)
    iota = lax.broadcasted_iota(jnp.int32, (8, 2 * LANES), 0)

    def pair(ref, h, i):
        lx, ys, lanes = i // (Y // 8), pl.ds(i % (Y // 8) * 8, 8), pl.ds(h * LANES, LANES)
        return jnp.concatenate([ref[2 * lx, ys, lanes], ref[2 * lx + 1, ys, lanes]], axis=1)

    def wide(v, s):
        return jnp.broadcast_to(v[s:s + 1], (8, 2 * LANES))

    def onehots(h):
        def step(i, unused):
            p = jnp.where(pair(cov, h, i) > 0, pair(pat, h, i), -1)
            phi, plo = p >> 4, p & 15
            for s in range(8):
                at = pl.ds(s * 2 * LANES, 2 * LANES)
                one = jnp.where(wide(phi, s) == iota, 1.0, 0.0)
                oh[h, i, :, at] = jnp.concatenate([one, one], axis=0).astype(BF16)
                lows = [jnp.where(wide(plo, s) == iota + k, 1.0, 0.0) for k in (0, 8)]
                rh[h, i, :, at] = jnp.concatenate(lows, axis=0).astype(BF16)
            return unused

        lax.fori_loop(0, X // 2 * (Y // 8), step, 0, unroll=2)

    def finish(h, alpha):
        lanes = pl.ds(h * LANES, LANES)

        def cstep(i, unused):
            x4 = pl.ds(i * 4, 4)
            both = jnp.concatenate(
                [yb[h, f, x4].reshape(4 * (Y + 2 * W), LANES) for f in range(2)], axis=1
            )
            high, low = split(both)
            kh = kyhi[...]
            val = dot(kh, high) + dot(kylo[...], high) + dot(kh, low)
            m = cov[x4, :, lanes].astype(F32).reshape(4 * Y, LANES)
            nbar = alpha * val[:, LANES:]
            weight = 1.0 / (1.0 + 2.0 * nbar)
            c = m * weight * (val[:, :LANES] / nbar - 1.0)
            contrast[x4, :, lanes] = c.reshape(4, Y, LANES)
            return unused

        lax.fori_loop(0, X // 4, cstep, 0, unroll=2)

        def pstep(i, unused):
            c = pair(contrast, h, i)
            terms = [oh[h, i]]
            power = c
            for q in range(3):
                high, low = split(power)
                high, low = high.astype(F32), low.astype(F32)
                terms.append(jnp.concatenate([
                    jnp.concatenate([wide(high, s), wide(low, s)], axis=0).astype(BF16)
                    for s in range(8)
                ], axis=1) * oh[h, i])
                power = power * c
            acc[...] += lax.dot_general(
                rh[h, i], jnp.concatenate(terms, axis=0), (((1,), (1,)), ((), ())),
                preferred_element_type=F32,
            )
            return unused

        lax.fori_loop(0, X // 2 * (Y // 8), pstep, 0, unroll=4)

    for h in range(halves):
        def xstep(t, unused):
            ys = pl.ds(t * 8, 8)
            both = jnp.concatenate(
                [xb[h, f, :, ys].reshape((X + 2 * W) * 8, LANES) for f in range(2)], axis=1
            )
            high, low = split(both)
            kh = kxhi[...]
            val = dot(kh, high) + dot(kxlo[...], high) + dot(kh, low)
            for f in range(2):
                yb[h, f, :, pl.ds(W + t * 8, 8)] = val[:, f * LANES:(f + 1) * LANES].reshape(X, 8, LANES)
            return unused

        if h == 0:
            relay_on(0)
            onehots(0)
        xarrived(h, 0)
        if h == 0:
            tcol[me_c] = add_up(row_totals, trow, rows)
            col_totals = gather_sum("col", cols, tcol, s2, r2)
        lax.fori_loop(0, W // 8, xstep, 0)

        @pl.when(me_c > 0)
        def _():
            ycopy(h, False).start()

        xarrived(h, 1)
        xsent(h)
        if h + 1 < halves:
            xstart(h + 1)
        lax.fori_loop(W // 8, Y // 8, xstep, 0)

        @pl.when(me_c < cols - 1)
        def _():
            ycopy(h, True).start()

        if h > 0:
            onehots(h)

        @pl.when(me_c > 0)
        def _():
            ycopy(h, True).wait_recv()

        @pl.when(me_c < cols - 1)
        def _():
            ycopy(h, False).wait_recv()

        if h + 1 < halves:
            relay_on(h + 1)
        if h == 0:
            tot = add_up(col_totals, tcol, cols)
            alpha = jnp.sum(tot[0], keepdims=True) / jnp.sum(tot[1], keepdims=True)
        finish(h, alpha)

    a = acc[...].T
    terms = [a[0:8]] + [a[16 * q:16 * q + 8] + a[16 * q + 8:16 * q + 16] for q in range(1, 4)]
    spread = jnp.dot(
        jnp.concatenate(terms, axis=0), rep[...],
        precision=lax.Precision.HIGHEST, preferred_element_type=F32,
    )
    patch_hi = lax.broadcasted_iota(jnp.int32, (8, NPATCH), 1) // 16
    own = patch_hi == lax.broadcasted_iota(jnp.int32, (8, NPATCH), 0)
    for q in range(4):
        part = jnp.where(own, spread[8 * q:8 * q + 8], 0.0)
        srow[me_r, q:q + 1] = jnp.sum(part, axis=0, keepdims=True)
    srow[me_r, 4:8] = jnp.zeros((4, NPATCH), F32)
    scol[me_c] = add_up(gather_sum("row", rows, srow, s3, r3), srow, rows)
    whole = add_up(gather_sum("col", cols, scol, s4, r4), scol, cols)
    sums[...] = whole[0:4] * scale

    for h in range(halves):
        relay(h, lambda copy: copy.wait_send())

        @pl.when(me_c > 0)
        def _():
            ycopy(h, False).wait_send()

        @pl.when(me_c < cols - 1)
        def _():
            ycopy(h, True).wait_send()


def local(galaxy, randoms, coverage, patch):
    rows, cols = lax.axis_size("row"), lax.axis_size("col")
    X, Y, Z = galaxy.shape
    halves = Z // LANES
    W = RADIUS
    scale = NPATCH / (X * rows * Y * cols * Z)
    tz = split_np(band(Z, Z, 0).T)
    kx = split_np(np.kron(band(X, X + 2 * W, W), np.eye(8, dtype=np.float32)))
    ky = split_np(np.kron(np.eye(4, dtype=np.float32), band(Y, Y + 2 * W, W)))
    rep = (np.arange(NPATCH)[None, :] % 16 == np.arange(16)[:, None]).astype(np.float32)
    consts = [jnp.asarray(v) for v in (*tz, *kx, *ky, rep)]
    args = (galaxy, randoms, coverage, patch, *consts)
    vmem = pl.BlockSpec(memory_space=pltpu.VMEM)
    dma = pltpu.SemaphoreType.DMA
    contrast, sums = pl.pallas_call(
        functools.partial(kernel, rows, cols, scale),
        out_shape=(
            jax.ShapeDtypeStruct((X, Y, Z), F32),
            jax.ShapeDtypeStruct((4, NPATCH), F32),
        ),
        in_specs=[pl.BlockSpec(memory_space=pl.ANY)] * 11,
        out_specs=(vmem, vmem),
        scratch_shapes=[pltpu.VMEM(v.shape, v.dtype) for v in args] + [
            pltpu.VMEM((halves, 2, X + 2 * W, Y, LANES), F32),
            pltpu.VMEM((halves, 2, X, Y + 2 * W, LANES), F32),
            pltpu.VMEM((16, 64), F32),
            pltpu.VMEM((rows, 2, 8, LANES), F32),
            pltpu.VMEM((cols, 2, 8, LANES), F32),
            pltpu.VMEM((rows, 8, NPATCH), F32),
            pltpu.VMEM((cols, 8, NPATCH), F32),
            pltpu.VMEM((halves, 2, W, Y // 2, LANES), F32),
            pltpu.VMEM((halves, X // 2 * (Y // 8), 16, 16 * LANES), BF16),
            pltpu.VMEM((halves, X // 2 * (Y // 8), 16, 16 * LANES), BF16),
            dma((11, X // 8)),
            dma((halves, 2, 2)), dma((halves, 2, 2)), dma((halves, 2)), dma((halves, 2)),
            dma((halves,)), dma((halves,)),
            dma((rows - 1,)), dma((rows - 1,)), dma((cols - 1,)), dma((cols - 1,)),
            dma((rows - 1,)), dma((rows - 1,)), dma((cols - 1,)), dma((cols - 1,)),
        ],
        compiler_params=pltpu.CompilerParams(
            collective_id=0, has_side_effects=True, vmem_limit_bytes=60 * 1024 * 1024
        ),
    )(*args)
    return contrast, sums


def solution(mesh):
    spec = P("row", "col", None)
    return jax.shard_map(
        local, mesh=mesh, in_specs=(spec,) * 4, out_specs=(spec, P()), check_vma=False
    )
```
